32 devices in a mesh: groups: 2 (over y), expert: 4 (over z), tensor: 2 (over x), inner: 2 (over core).
Axes of the slice: x: 2, y: 2, z: 4, core: 2. Of those that a mesh axis runs over, the one named last changes fastest.
Arguments:
- tokens: bfloat16 [1024, 7168], P(('groups', 'expert'), ('tensor', 'inner')), parts along dimension 0, may hold values from -6 to 6
- expert_ids: int32 [1024, 8], P(('groups', 'expert')), parts along dimension 0, may hold values from 0 to 31, all different within a row; in each aligned block of 128 rows (0 to 127, 128 to 255, ...) at most 96 rows name the same one
- gate_weights: float32 [1024, 8], P(('groups', 'expert')), parts along dimension 0, may hold values from 0.05 to 0.45
- base_weights: bfloat16 [3, 1024, 7168], P(None, 'expert', ('tensor', 'inner')), may hold values from -0.0625 to 0.0625
- in_factor: bfloat16 [3840, 7168], P('expert', ('tensor', 'inner')), may hold values from -0.0625 to 0.0625
- out_factors: bfloat16 [2, 3840, 1024], P(None, 'expert', ('tensor', 'inner')), may hold values from -0.375 to 0.375
- ranks: int32 [32], P('expert'), may hold values from 64 to 512, as said below
Outputs:
- mixed: bfloat16 [1024, 7168], P(('groups', 'expert'), ('tensor', 'inner')), parts along dimension 0
The draws below stay inside these ranges and needn't reach their ends.
There are 2 independent parts, one for each index of `groups`. The reference program is written for one: setup_inputs(seed, part) draws one part's arguments, and reference() takes and returns one part's arrays. A program takes and returns all parts, laid end to end along the dimension named above; an argument that names none is the same for every part. Nothing has to cross between parts.
Inputs may be any that keep to these rules, and one draw needn't show every extreme that they name: `expert_ids`: in each aligned block of 128 tokens no expert is chosen more than 96 times, and some expert is chosen exactly 96 times; the experts of one token differ. The ranks of each aligned block of 8 experts sum to exactly 960.
All inputs are finite; a program needn't handle non-finite values.
Results may differ from the reference program's by a relative error of at most 0.023.
Values may be sent and summed in bfloat16 or wider, within the bound.
A program may use at most 64 MiB of HBM per device.

```python
import math
import jax
import jax.numpy as jnp
import numpy as np
from jax import lax

D = 7168
F = 1024
TOP = 8
EXP_DEV = 8
TOK_E = 128
RANK_MIN = 64
RANK_MAX = 512
EXPERTS = 32
TOKENS = 512
CAP = 96
RANKS_ALL = 3840
N_EXPERT = 4
N_TENSOR = 2
N_INNER = 2


def draw_ranks(key, part):
    groups_count = EXPERTS // EXP_DEV
    extra = RANK_MAX - RANK_MIN
    first, second, third = jax.random.split(key, 3)
    cuts = jnp.sort(jax.random.randint(first, (groups_count, EXP_DEV - 1), 0, extra + 1), axis=1)
    edges = jnp.concatenate([jnp.zeros((groups_count, 1), jnp.int32), cuts.astype(jnp.int32), jnp.full((groups_count, 1), extra, jnp.int32)], 1)
    shares = edges[:, 1:] - edges[:, :-1]
    chosen = jax.random.randint(second, (), 0, groups_count)
    single = jax.random.randint(third, (), 0, EXP_DEV)
    forced = jnp.where(jnp.arange(EXP_DEV) == single, extra, 0).astype(jnp.int32)
    shares = jnp.where((jnp.arange(groups_count) == chosen)[:, None], forced[None, :], shares)
    return (RANK_MIN + shares).reshape(EXPERTS).astype(jnp.int32)


def level_of(own_key, shape, cuts, least, top_value):
    loudness = 1.0
    for axis_at, blocks in cuts:
        draws = jax.random.uniform(jax.random.fold_in(jax.random.fold_in(own_key, 6), axis_at), (blocks,), jnp.float32, least / len(cuts), top_value / len(cuts))
        loudness = loudness * jnp.repeat(jnp.exp(draws), shape[axis_at] // blocks).reshape((-1,) + (1,) * (len(shape) - 1 - axis_at))
    return loudness


def deal_out(key, own, number, rows, count, top, bound, slope):
    ranking = jax.random.permutation(key, count)
    packed, usual = load_shares(count, rows * top, bound, slope, True), load_shares(count, rows * top, bound, slope, False)
    places = jnp.arange(count)

    def named(sizes, turn):
        used = int((sizes > 0).sum())
        fixed = max(1, used // 4)
        passed = fixed + (places - fixed + turn * (used - fixed)) % max(1, count - fixed)
        return jnp.zeros((count,), jnp.int32).at[ranking[jnp.where(places < fixed, places, passed)]].set(jnp.asarray(sizes, jnp.int32))

    sizes = jnp.where(number % 4 == 0, named(packed, number // 4), named(usual, number - number // 4 - 1))
    mixed = jax.random.permutation(jax.random.fold_in(own, 3), count)
    donor, receiver = mixed[0:count // 2 * 2:2], mixed[1:count // 2 * 2:2]
    slack = jnp.minimum(sizes[donor] - 1, bound - sizes[receiver]) // 2
    slack = jnp.where((donor == ranking[0]) | (receiver == ranking[0]) | (sizes[receiver] == 0), 0, jnp.maximum(slack, 0))
    passed = jax.random.randint(jax.random.fold_in(own, 4), (count // 2,), 0, 1 << 20) % (slack + 1)
    sizes = sizes.at[donor].add(-passed).at[receiver].add(passed)
    items = jnp.searchsorted(jnp.cumsum(sizes), jnp.arange(rows * top), side="right").astype(jnp.int32)
    listing = items.reshape(top, rows).T
    listing = listing[jax.random.permutation(jax.random.fold_in(own, 1), rows)]
    turn = jax.random.randint(jax.random.fold_in(own, 2), (rows, 1), 0, top)
    return jnp.take_along_axis(listing, (jnp.arange(top)[None, :] + turn) % top, axis=1)


def load_shares(amount, total, reach, skew, full):
    weights = [(1 << 20) // math.isqrt(rank ** skew) + 1 for rank in range(1, amount + 1)]
    largest = reach if full else min(reach, max(-(-total // amount), total * weights[0] // sum(weights)))
    least = 1 if total - largest >= amount - 1 else 0
    given, rest = [largest] + [least] * (amount - 1), total - largest - least * (amount - 1)
    while rest > 0:
        free = [i for i in range(1, amount) if given[i] < largest] or [i for i in range(1, amount) if given[i] < reach]
        pool, remaining = sum([weights[i] for i in free]), rest
        for i in free:
            more = min(reach - given[i], max(1, remaining * weights[i] // pool), rest)
            given[i] = given[i] + more
            rest = rest - more
    return np.array(given)


def gaussian(rng, extent, width, bound, cuts=(), kind=jnp.bfloat16):
    drawn = width * jax.random.normal(rng, extent, jnp.float32)
    if cuts:
        drawn = drawn * level_of(rng, extent, cuts, -0.22, 0.18)
    return jnp.clip(drawn, -bound, bound).astype(kind)


def setup_inputs(seed: int = 0, part: int = 0) -> dict:
    streams_of = jax.random.split(jax.random.key(seed), 8)
    own_keys = jax.random.split(jax.random.fold_in(streams_of[7], part), 8)
    tokens = gaussian(own_keys[0], (TOKENS, D), 1.0, 6.0, ((0, 4), (1, 4)))
    expert_ids_keys = jax.random.split(jax.random.fold_in(own_keys[1], 1), TOKENS // TOK_E)
    expert_ids_turns = jax.random.permutation(jax.random.fold_in(own_keys[1], 3), TOKENS // TOK_E)
    expert_ids = jax.vmap(lambda own, number: deal_out(jax.random.fold_in(own_keys[1], 2), own, number, TOK_E, EXPERTS, TOP, CAP, 2))(expert_ids_keys, expert_ids_turns).reshape((TOKENS, TOP))
    gate_weights = jnp.clip(0.05 + 0.39999999 * jax.random.uniform(own_keys[2], (TOKENS, TOP), jnp.float32) ** level_of(own_keys[2], (TOKENS, TOP), ((0, 4),), -0.2, 0.2), 0.05, 0.45)
    base_weights = gaussian(streams_of[3], (3, F, D), D ** -0.5, 0.0625, ((1, 4), (2, 4)))
    in_factor = gaussian(streams_of[4], (RANKS_ALL, D), D ** -0.5, 0.0625, ((0, 4), (1, 4)))
    out_factors = gaussian(streams_of[5], (2, RANKS_ALL, F), (RANK_MAX // 2) ** -0.5, 0.375, ((1, 4), (2, 4)))
    ranks = draw_ranks(jax.random.fold_in(streams_of[7], 71), part)
    return dict(tokens=tokens, expert_ids=expert_ids, gate_weights=gate_weights, base_weights=base_weights, in_factor=in_factor, out_factors=out_factors, ranks=ranks)


def reference(tokens, expert_ids, gate_weights, base_weights, in_factor, out_factors, ranks):
    blocks_count = N_TENSOR * N_INNER
    pieces = D // blocks_count
    rows_per = N_EXPERT * CAP
    base_rows = jnp.einsum("td,gfd->tgf", tokens.astype(jnp.float32), base_weights[:2].astype(jnp.float32)).astype(jnp.bfloat16)
    start = (jnp.cumsum(ranks) - ranks).astype(jnp.int32)
    pairs = TOKENS * TOP
    flat_ids = expert_ids.reshape(pairs).astype(jnp.int32)
    onehot = (flat_ids[:, None] == jnp.arange(EXPERTS, dtype=jnp.int32)[None, :]).astype(jnp.int32)
    onehot = onehot.reshape(N_EXPERT, TOK_E * TOP, EXPERTS)
    before = jnp.cumsum(onehot, axis=1) - onehot
    slot = jnp.sum(before * onehot, axis=2).reshape(pairs).astype(jnp.int32)
    block_of = (jnp.arange(pairs, dtype=jnp.int32) // (TOK_E * TOP)).astype(jnp.int32)
    target = (flat_ids * rows_per + block_of * CAP + slot).astype(jnp.int32)
    table = jnp.full((EXPERTS * rows_per,), -1, jnp.int32).at[target].set(jnp.arange(pairs, dtype=jnp.int32))
    table = table.reshape(EXPERTS, rows_per)
    in_pad = jnp.concatenate([in_factor, jnp.zeros((RANK_MAX, D), in_factor.dtype)], 0)
    out_pad = jnp.concatenate([out_factors, jnp.zeros((2, RANK_MAX, F), out_factors.dtype)], 1)
    within = jnp.arange(RANK_MAX, dtype=jnp.int32)

    def one_expert(expert):
        index = table[expert]
        valid = index >= 0
        source = (jnp.maximum(index, 0) // TOP).astype(jnp.int32)
        routed = jnp.where(valid[:, None], tokens[source], jnp.zeros((), tokens.dtype)).astype(jnp.float32)
        window = lax.dynamic_slice_in_dim(in_pad, start[expert], RANK_MAX, 0).astype(jnp.float32)
        parts = jnp.einsum("rpd,cpd->prc", routed.reshape(rows_per, blocks_count, pieces), window.reshape(RANK_MAX, blocks_count, pieces))
        rounded = lax.optimization_barrier(parts.astype(jnp.bfloat16))
        latent = jnp.sum(rounded.astype(jnp.float32), axis=0)
        latent = jnp.where(within[None, :] < ranks[expert], latent, jnp.float32(0.0)).astype(jnp.bfloat16)
        factor = lax.dynamic_slice_in_dim(out_pad, start[expert], RANK_MAX, 1).astype(jnp.float32)
        return jnp.einsum("rc,gcf->rgf", latent.astype(jnp.float32), factor).astype(jnp.bfloat16)

    deltas = lax.map(one_expert, jnp.arange(EXPERTS, dtype=jnp.int32))
    picked = deltas.reshape(EXPERTS * rows_per, 2, F)[target].reshape(TOKENS, TOP, 2, F)
    summed = base_rows.astype(jnp.float32)[:, None] + picked.astype(jnp.float32)
    hidden = (jax.nn.silu(summed[:, :, 0]) * summed[:, :, 1]).astype(jnp.bfloat16)
    combined = jnp.sum(gate_weights[:, :, None] * hidden.astype(jnp.float32), axis=1).astype(jnp.bfloat16)
    return jnp.dot(combined, base_weights[2], preferred_element_type=jnp.float32).astype(jnp.bfloat16)
```

```python
import jax
import jax.numpy as jnp
from jax import lax
from jax.sharding import PartitionSpec as P

FEATURE_AXES = ("tensor", "inner")


def on_device(tokens, expert_ids, gate_weights, base_weights, in_factor, out_factors, ranks):
    tok_rows, feat_slice = tokens.shape
    owners = lax.axis_size("expert")
    local_count = ranks.shape[0]
    experts = local_count * owners
    packed = in_factor.shape[0]
    hidden_rows = base_weights.shape[1]
    hidden_slice = out_factors.shape[2]
    rows = tok_rows * owners

    all_tokens = lax.all_gather(tokens, "expert", axis=0, tiled=True)
    down = lax.all_gather(base_weights[2], "expert", axis=0, tiled=True)

    columns = lax.broadcasted_iota(jnp.int32, (1, 1, experts), 2)
    chosen = expert_ids[:, :, None] == columns
    dense_gates = jnp.sum(jnp.where(chosen, gate_weights[:, :, None], 0.0), axis=1)
    all_gates = lax.all_gather(dense_gates, "expert", axis=0, tiled=True)
    own_gates = lax.dynamic_slice_in_dim(
        all_gates, lax.axis_index("expert") * local_count, local_count, 1
    )

    latent_part = lax.dot_general(
        all_tokens, in_factor, (((1,), (1,)), ((), ())), preferred_element_type=jnp.float32
    ).astype(jnp.bfloat16)
    latent = lax.psum(latent_part, FEATURE_AXES)

    base_part = lax.dot_general(
        all_tokens,
        base_weights[:2].reshape(2 * hidden_rows, feat_slice),
        (((1,), (1,)), ((), ())),
        preferred_element_type=jnp.float32,
    ).astype(jnp.bfloat16)
    base = lax.psum_scatter(base_part, FEATURE_AXES, scatter_dimension=0, tiled=True)
    base = base.reshape(-1, 2, hidden_rows)
    base = lax.all_gather(base, "expert", axis=2, tiled=True)
    base = lax.all_to_all(base, FEATURE_AXES, split_axis=2, concat_axis=0, tiled=True)
    gate_rows = base[:, 0].astype(jnp.float32)
    up_rows = base[:, 1].astype(jnp.float32)

    order = lax.broadcasted_iota(jnp.int32, (local_count, local_count), 0)
    other = lax.broadcasted_iota(jnp.int32, (local_count, local_count), 1)
    ends = jnp.sum(jnp.where(other <= order, ranks[None, :], 0), axis=1)
    where = lax.broadcasted_iota(jnp.int32, (1, packed), 1)
    combined = jnp.zeros((rows, hidden_slice), jnp.float32)
    for member in range(local_count):
        inside = (where >= ends[member] - ranks[member]) & (where < ends[member])
        own = jnp.where(inside, latent, jnp.zeros((), jnp.bfloat16))
        gate = jnp.dot(own, out_factors[0], preferred_element_type=jnp.float32)
        up = jnp.dot(own, out_factors[1], preferred_element_type=jnp.float32)
        hidden = jax.nn.silu(gate_rows + gate) * (up_rows + up)
        combined = combined + own_gates[:, member : member + 1] * hidden
    combined = lax.psum_scatter(
        combined.astype(jnp.bfloat16), "expert", scatter_dimension=0, tiled=True
    )
    full_hidden = lax.all_gather(combined, FEATURE_AXES, axis=1, tiled=True)
    return jnp.dot(full_hidden, down, preferred_element_type=jnp.float32).astype(jnp.bfloat16)


def solution(mesh):
    return jax.shard_map(
        on_device,
        mesh=mesh,
        in_specs=(
            P(("groups", "expert"), ("tensor", "inner")),
            P(("groups", "expert"), None),
            P(("groups", "expert"), None),
            P(None, "expert", ("tensor", "inner")),
            P("expert", ("tensor", "inner")),
            P(None, "expert", ("tensor", "inner")),
            P("expert"),
        ),
        out_specs=P(("groups", "expert"), ("tensor", "inner")),
        check_vma=False,
    )
```

```python
import functools
import jax
import jax.numpy as jnp
from jax import lax
from jax.experimental import pallas as pl
from jax.experimental.pallas import tpu as pltpu
from jax.sharding import PartitionSpec as P

FEATURE_AXES = ("tensor", "inner")
MESH = pl.DeviceIdType.MESH
BF16 = jnp.bfloat16
F32 = jnp.float32


def nearest(at, k, n):
    both = jnp.minimum(at, n - 1 - at)
    near = (k + 1) // 2
    left_near = k % 2
    far = k - both
    left_far = (at > n - 1 - at).astype(jnp.int32)
    inside = (k <= 2 * both).astype(jnp.int32)
    dist = inside * near + (1 - inside) * far
    left = inside * left_near + (1 - inside) * left_far
    return at + dist * (1 - 2 * left)


def fused(
    n, plane, tokens, gates, mask, base_weights, in_factor, out_factors, out,
    all_tok, base_w, in_w, out_w, own_gates, part, a_got, half, bl_got, bb_got, lat, piece,
    base_all, delta, comb, comb_got, full,
    load_sem, tok_l, tok_r, tok_got, gate_s, gate_r, a_s, a_r, bl_s, bl_r, bb_s, bb_r, c_s, c_r,
    base_s, base_r, comb_s, comb_r, ag_s, ag_r,
):
    me = lax.axis_index("expert")
    x = lax.axis_index("tensor")
    c = lax.axis_index("inner")
    ti = x * 2 + c
    rows = tokens.shape[0]
    packed = in_factor.shape[0]
    wide = bl_got.shape[2]
    unit = base_weights.shape[1]
    local = mask.shape[0]
    hid = out_factors.shape[2]
    two, four = rows // 2, rows // 4

    def rdma(src, dst, send, recv, **where):
        return pltpu.make_async_remote_copy(
            src_ref=src, dst_ref=dst, send_sem=send, recv_sem=recv,
            device_id=where, device_id_type=MESH,
        )

    barrier = pltpu.get_barrier_semaphore()
    for de in range(n):
        for dt in range(plane):
            if de or dt:
                to = lax.rem(ti + dt, plane)
                pl.semaphore_signal(
                    barrier, inc=1,
                    device_id={"expert": lax.rem(me + de, n), "tensor": to // 2, "inner": lax.rem(to, 2)},
                    device_id_type=MESH,
                )
    loads = [
        pltpu.make_async_copy(tokens, all_tok.at[me], load_sem.at[0]),
        pltpu.make_async_copy(in_factor, in_w, load_sem.at[1]),
        pltpu.make_async_copy(base_weights.at[pl.ds(0, 2)], base_w, load_sem.at[2]),
        pltpu.make_async_copy(out_factors, out_w, load_sem.at[3]),
        pltpu.make_async_copy(
            gates.at[pl.ds(pl.multiple_of(me * local, local), local)], own_gates.at[me], load_sem.at[4]
        ),
    ]
    for load in loads:
        load.start()
    pl.semaphore_wait(barrier, n * plane - 1)

    def to_right(b, src):
        return rdma(src, all_tok.at[b], tok_r.at[b], tok_got.at[b], expert=lax.rem(me + 1, n))

    def to_left(b, src):
        return rdma(src, all_tok.at[b], tok_l.at[b], tok_got.at[b], expert=lax.rem(me + n - 1, n))

    @pl.when(me + 1 < n)
    def _():
        to_right(me, tokens).start()

    @pl.when(me >= 1)
    def _():
        to_left(me, tokens).start()

    def gate_copy(step):
        p = lax.rem(me + step, n)
        return rdma(
            gates.at[pl.ds(pl.multiple_of(p * local, local), local)], own_gates.at[me],
            gate_s.at[p], gate_r.at[me], expert=p,
        )

    for step in range(1, n):
        gate_copy(step).start()

    mine = pl.multiple_of(c * two, two)
    other = pl.multiple_of((1 - c) * two, two)

    def a_copy(b):
        return rdma(part.at[b, pl.ds(other, two)], a_got.at[b], a_s.at[b], a_r.at[b], inner=1 - c)

    def bl_copy(b):
        return rdma(
            half.at[b, :, pl.ds(0, wide)], bl_got.at[b], bl_s.at[b], bl_r.at[b], tensor=1 - x
        )

    def bb_copy(b):
        return rdma(
            half.at[b, pl.ds(pl.multiple_of((1 - x) * four, four), four), pl.ds(wide, 2 * unit)],
            bb_got.at[b], bb_s.at[b], bb_r.at[b], tensor=1 - x,
        )

    def c_copy(b):
        return rdma(lat.at[b, pl.ds(mine, two)], lat.at[b, pl.ds(mine, two)], c_s.at[b], c_r.at[b], inner=1 - c)

    quarter = c * 2 + x

    def base_copy(b, e):
        return rdma(
            piece.at[b], base_all.at[b, pl.ds(pl.multiple_of(quarter * four, four), four)],
            base_s.at[b, e], base_r.at[b, quarter], expert=e, tensor=me // 2, inner=lax.rem(me, 2),
        )

    for load in loads:
        load.wait()

    def phase(k, carry):
        b = nearest(me, jnp.minimum(k, n - 1), n)

        @pl.when(k < n)
        def _():
            @pl.when(k >= 1)
            def _():
                to_right(b, all_tok.at[b]).wait_recv()

                @pl.when((b < me) & (me + 1 < n))
                def _():
                    to_right(b, all_tok.at[b]).start()

                @pl.when((b > me) & (me >= 1))
                def _():
                    to_left(b, all_tok.at[b]).start()

            t = all_tok[b]
            nt = (((1,), (1,)), ((), ()))
            value = lax.dot_general(t, in_w[...], nt, preferred_element_type=F32).astype(BF16)
            if wide > packed:
                part[b, :, packed:wide] = jnp.zeros((rows, wide - packed), BF16)
            part[b, :, 0:packed] = value
            for g in range(2):
                value = lax.dot_general(t, base_w[g], nt, preferred_element_type=F32)
                part[b, :, wide + g * unit : wide + (g + 1) * unit] = value.astype(BF16)
            a_copy(b).start()

        @pl.when((k >= 1) & (k <= n))
        def _():
            p = nearest(me, jnp.maximum(k - 1, 0), n)
            bb_copy(p).wait_recv()
            own = half[p, pl.ds(pl.multiple_of(x * four, four), four), wide : wide + 2 * unit]
            piece[p] = (own.astype(F32) + bb_got[p].astype(F32)).astype(BF16)
            for e in range(n):
                here = (me == e) & (ti == me)

                @pl.when(jnp.logical_not(here))
                def _():
                    base_copy(p, e).start()

                @pl.when(here)
                def _():
                    base_all[p, pl.ds(pl.multiple_of(quarter * four, four), four)] = piece[p]

            bl_copy(p).wait_recv()
            lat[p, pl.ds(mine, two)] = (
                half[p, :, 0:wide].astype(F32) + bl_got[p].astype(F32)
            ).astype(BF16)
            c_copy(p).start()

        @pl.when(k < n)
        def _():
            a_copy(b).wait_recv()
            half[b] = (part[b, pl.ds(mine, two)].astype(F32) + a_got[b].astype(F32)).astype(BF16)
            bb_copy(b).start()
            bl_copy(b).start()

        @pl.when(k >= 2)
        def _():
            p = nearest(me, jnp.maximum(k - 2, 0), n)
            rdma(
                lat.at[p, pl.ds(other, two)], lat.at[p, pl.ds(other, two)], c_s.at[p], c_r.at[p],
                inner=1 - c,
            ).wait_recv()
            value = lat[p, :, 0:packed]
            for j in range(local):
                own = value * mask[j : j + 1, :].astype(BF16)
                for g in range(2):
                    delta[p, j, :, g * hid : (g + 1) * hid] = jnp.dot(
                        own, out_w[g], preferred_element_type=F32
                    ).astype(BF16)

        return carry

    lax.fori_loop(0, n + 2, phase, 0)

    for step in range(1, n):
        p = lax.rem(me + step, n)
        rdma(own_gates.at[p], own_gates.at[p], gate_s.at[p], gate_r.at[p], expert=p).wait_recv()

    def comb_copy(b):
        return rdma(comb.at[b], comb_got.at[me], comb_s.at[b], comb_r.at[me], expert=b)

    def finish(k, carry):
        b = nearest(ti, k, n)
        for q in range(plane):
            @pl.when(jnp.logical_not((me == ti) & (quarter == q)))
            def _():
                spot = base_all.at[b, pl.ds(q * four, four)]
                rdma(spot, spot, base_s.at[b, 0], base_r.at[b, q], tensor=1 - x).wait_recv()

        pick = (
            lax.broadcasted_iota(jnp.int32, (local, 128), 0)
            == lax.broadcasted_iota(jnp.int32, (local, 128), 1)
        ).astype(F32)
        weight = lax.dot_general(
            own_gates[b], pick, (((0,), (0,)), ((), ())),
            preferred_element_type=F32, precision=lax.Precision.HIGHEST,
        )
        gate_base = base_all[b, :, 0:unit].astype(F32)
        up_base = base_all[b, :, unit : 2 * unit].astype(F32)
        total = jnp.zeros((rows, hid), F32)
        for j in range(local):
            v = gate_base + delta[b, j, :, 0:hid].astype(F32)
            u = up_base + delta[b, j, :, hid : 2 * hid].astype(F32)
            total = total + weight[:, j : j + 1] * (v / (1.0 + jnp.exp(-v)) * u)
        comb[b] = total.astype(BF16)

        @pl.when(b != me)
        def _():
            comb_copy(b).start()

        return carry

    lax.fori_loop(0, n, finish, 0)

    total = comb[me].astype(F32)
    for step in range(1, n):
        p = lax.rem(me + step, n)
        rdma(comb_got.at[p], comb_got.at[p], comb_s.at[p], comb_r.at[p], expert=p).wait_recv()
        total = total + comb_got[p].astype(F32)
    full[ti] = total.astype(BF16)

    def ag_copy(step):
        to = lax.rem(ti + step, plane)
        return rdma(
            full.at[ti], full.at[ti], ag_s.at[to], ag_r.at[ti], tensor=to // 2, inner=lax.rem(to, 2)
        )

    for step in range(1, plane):
        ag_copy(step).start()
    for step in range(1, plane):
        p = lax.rem(ti + step, plane)
        rdma(full.at[p], full.at[p], ag_s.at[p], ag_r.at[p], tensor=1 - x).wait_recv()
    for q in range(plane):
        out[:, q * hid : (q + 1) * hid] = full[q]

    for b in range(n):
        @pl.when((b <= me) & (me + 1 < n))
        def _():
            to_right(b, all_tok.at[b]).wait_send()

        @pl.when((b >= me) & (me >= 1))
        def _():
            to_left(b, all_tok.at[b]).wait_send()

        a_copy(b).wait_send()
        bl_copy(b).wait_send()
        bb_copy(b).wait_send()
        c_copy(b).wait_send()
        for e in range(n):
            @pl.when(jnp.logical_not((me == e) & (ti == me)))
            def _():
                base_copy(b, e).wait_send()

        @pl.when(b != me)
        def _():
            comb_copy(b).wait_send()

    for step in range(1, n):
        gate_copy(step).wait_send()
    for step in range(1, plane):
        ag_copy(step).wait_send()


def hidden_of(tokens, dense_gates, base_weights, in_factor, out_factors, ranks):
    rows, feat = tokens.shape
    n = lax.axis_size("expert")
    plane = lax.axis_size("tensor") * lax.axis_size("inner")
    local = ranks.shape[0]
    packed = in_factor.shape[0]
    wide = -(-packed // 128) * 128
    unit = base_weights.shape[1]
    hid = out_factors.shape[2]
    order = lax.broadcasted_iota(jnp.int32, (local, local), 0)
    other = lax.broadcasted_iota(jnp.int32, (local, local), 1)
    ends = jnp.sum(jnp.where(other <= order, ranks[None, :], 0), axis=1)[:, None]
    place = lax.broadcasted_iota(jnp.int32, (local, packed), 1)
    mask = ((place < ends) & (place >= ends - ranks[:, None])).astype(F32)
    two, four = rows // 2, rows // 4
    vmem = pltpu.VMEM
    dma = pltpu.SemaphoreType.DMA
    return pl.pallas_call(
        functools.partial(fused, n, plane),
        out_shape=jax.ShapeDtypeStruct((rows, plane * hid), BF16),
        in_specs=[
            pl.BlockSpec(memory_space=pl.ANY),
            pl.BlockSpec(memory_space=vmem),
            pl.BlockSpec(memory_space=vmem),
            pl.BlockSpec(memory_space=pl.ANY),
            pl.BlockSpec(memory_space=pl.ANY),
            pl.BlockSpec(memory_space=pl.ANY),
        ],
        out_specs=pl.BlockSpec(memory_space=vmem),
        scratch_shapes=[
            vmem((n, rows, feat), BF16),
            vmem((2, unit, feat), BF16),
            vmem((packed, feat), BF16),
            vmem((2, packed, hid), BF16),
            vmem((n, local, rows), F32),
            vmem((n, rows, wide + 2 * unit), BF16),
            vmem((n, two, wide + 2 * unit), BF16),
            vmem((n, two, wide + 2 * unit), BF16),
            vmem((n, two, wide), BF16),
            vmem((n, four, 2 * unit), BF16),
            vmem((n, rows, wide), BF16),
            vmem((n, four, 2 * unit), BF16),
            vmem((n, rows, 2 * unit), BF16),
            vmem((n, local, rows, 2 * hid), BF16),
            vmem((n, rows, hid), BF16),
            vmem((n, rows, hid), BF16),
            vmem((plane, rows, hid), BF16),
            dma((5,)),
            dma((n,)), dma((n,)), dma((n,)), dma((n,)), dma((n,)),
            dma((n,)), dma((n,)), dma((n,)), dma((n,)), dma((n,)), dma((n,)), dma((n,)), dma((n,)),
            dma((n, n)), dma((n, plane)), dma((n,)), dma((n,)), dma((plane,)), dma((plane,)),
        ],
        compiler_params=pltpu.CompilerParams(
            collective_id=0, has_side_effects=True, vmem_limit_bytes=48 * 1024 * 1024
        ),
        cost_estimate=pl.CostEstimate(
            flops=60_000_000_000, bytes_accessed=20_000_000, transcendentals=0
        ),
    )(tokens, dense_gates.T, mask, base_weights, in_factor, out_factors)


def on_device(tokens, expert_ids, gate_weights, base_weights, in_factor, out_factors, ranks):
    tok_rows, feat_slice = tokens.shape
    owners = lax.axis_size("expert")
    local_count = ranks.shape[0]
    experts = local_count * owners
    packed = in_factor.shape[0]
    hidden_rows = base_weights.shape[1]
    hidden_slice = out_factors.shape[2]
    rows = tok_rows * owners

    down = lax.all_gather(base_weights[2], "expert", axis=0, tiled=True)

    columns = lax.broadcasted_iota(jnp.int32, (1, 1, experts), 2)
    chosen = expert_ids[:, :, None] == columns
    dense_gates = jnp.sum(jnp.where(chosen, gate_weights[:, :, None], 0.0), axis=1)
    tensor, inner = lax.axis_size("tensor"), lax.axis_size("inner")
    if tensor == 2 and inner == 2 and owners == tensor * inner and tok_rows % 64 == 0:
        full_hidden = hidden_of(
            tokens, dense_gates, base_weights, in_factor, out_factors, ranks
        )
        return jnp.dot(full_hidden, down, preferred_element_type=jnp.float32).astype(jnp.bfloat16)
    all_tokens = lax.all_gather(tokens, "expert", axis=0, tiled=True)
    all_gates = lax.all_gather(dense_gates, "expert", axis=0, tiled=True)
    own_gates = lax.dynamic_slice_in_dim(
        all_gates, lax.axis_index("expert") * local_count, local_count, 1
    )

    latent_part = lax.dot_general(
        all_tokens, in_factor, (((1,), (1,)), ((), ())), preferred_element_type=jnp.float32
    ).astype(jnp.bfloat16)
    latent = lax.psum(latent_part, FEATURE_AXES)

    base_part = lax.dot_general(
        all_tokens,
        base_weights[:2].reshape(2 * hidden_rows, feat_slice),
        (((1,), (1,)), ((), ())),
        preferred_element_type=jnp.float32,
    ).astype(jnp.bfloat16)
    base = lax.psum_scatter(base_part, FEATURE_AXES, scatter_dimension=0, tiled=True)
    base = base.reshape(-1, 2, hidden_rows)
    base = lax.all_gather(base, "expert", axis=2, tiled=True)
    base = lax.all_to_all(base, FEATURE_AXES, split_axis=2, concat_axis=0, tiled=True)
    gate_rows = base[:, 0].astype(jnp.float32)
    up_rows = base[:, 1].astype(jnp.float32)

    order = lax.broadcasted_iota(jnp.int32, (local_count, local_count), 0)
    other = lax.broadcasted_iota(jnp.int32, (local_count, local_count), 1)
    ends = jnp.sum(jnp.where(other <= order, ranks[None, :], 0), axis=1)
    where = lax.broadcasted_iota(jnp.int32, (1, packed), 1)
    combined = jnp.zeros((rows, hidden_slice), jnp.float32)
    for member in range(local_count):
        inside = (where >= ends[member] - ranks[member]) & (where < ends[member])
        own = jnp.where(inside, latent, jnp.zeros((), jnp.bfloat16))
        gate = jnp.dot(own, out_factors[0], preferred_element_type=jnp.float32)
        up = jnp.dot(own, out_factors[1], preferred_element_type=jnp.float32)
        hidden = jax.nn.silu(gate_rows + gate) * (up_rows + up)
        combined = combined + own_gates[:, member : member + 1] * hidden
    combined = lax.psum_scatter(
        combined.astype(jnp.bfloat16), "expert", scatter_dimension=0, tiled=True
    )
    full_hidden = lax.all_gather(combined, FEATURE_AXES, axis=1, tiled=True)
    return jnp.dot(full_hidden, down, preferred_element_type=jnp.float32).astype(jnp.bfloat16)


def solution(mesh):
    return jax.shard_map(
        on_device,
        mesh=mesh,
        in_specs=(
            P(("groups", "expert"), ("tensor", "inner")),
            P(("groups", "expert"), None),
            P(("groups", "expert"), None),
            P(None, "expert", ("tensor", "inner")),
            P("expert", ("tensor", "inner")),
            P(None, "expert", ("tensor", "inner")),
            P("expert"),
        ),
        out_specs=P(("groups", "expert"), ("tensor", "inner")),
        check_vma=False,
    )
```

```python
import functools
import jax
import jax.numpy as jnp
from jax import lax
from jax.experimental import pallas as pl
from jax.experimental.pallas import tpu as pltpu
from jax.sharding import PartitionSpec as P

FEATURE_AXES = ("tensor", "inner")
MESH = pl.DeviceIdType.MESH
BF16 = jnp.bfloat16
F32 = jnp.float32


def nearest(at, k, n):
    both = jnp.minimum(at, n - 1 - at)
    near = (k + 1) // 2
    left_near = k % 2
    far = k - both
    left_far = (at > n - 1 - at).astype(jnp.int32)
    inside = (k <= 2 * both).astype(jnp.int32)
    dist = inside * near + (1 - inside) * far
    left = inside * left_near + (1 - inside) * left_far
    return at + dist * (1 - 2 * left)


def fused(
    n, plane, tokens, gates, mask, base_weights, in_factor, out_factors, out,
    all_tok, base_w, in_w, out_w, own_gates, part, a_got, half, bl_got, bb_got, lat, piece,
    base_all, delta, comb, comb_got, full, down_w, acc,
    load_sem, tok_l, tok_r, tok_got, gate_s, gate_r, a_s, a_r, bl_s, bl_r, bb_s, bb_r, c_s, c_r,
    base_s, base_r, comb_s, comb_r, ag_s, ag_r, wl_s, wr_s, w_got, wy_s, wy_got,
):
    me = lax.axis_index("expert")
    x = lax.axis_index("tensor")
    c = lax.axis_index("inner")
    y = lax.axis_index("groups")
    ti = x * 2 + c
    cuts = w_got.shape[1]
    rows = tokens.shape[0]
    packed = in_factor.shape[0]
    wide = bl_got.shape[2]
    unit = base_weights.shape[1]
    local = mask.shape[0]
    hid = out_factors.shape[2]
    two, four = rows // 2, rows // 4

    def rdma(src, dst, send, recv, **where):
        return pltpu.make_async_remote_copy(
            src_ref=src, dst_ref=dst, send_sem=send, recv_sem=recv,
            device_id=where, device_id_type=MESH,
        )

    barrier = pltpu.get_barrier_semaphore()
    for de in range(n):
        for dt in range(plane):
            if de or dt:
                to = lax.rem(ti + dt, plane)
                pl.semaphore_signal(
                    barrier, inc=1,
                    device_id={"expert": lax.rem(me + de, n), "tensor": to // 2, "inner": lax.rem(to, 2)},
                    device_id_type=MESH,
                )
    pl.semaphore_signal(barrier, inc=1, device_id={"groups": 1 - y}, device_id_type=MESH)
    loads = [
        pltpu.make_async_copy(tokens, all_tok.at[me], load_sem.at[0]),
        pltpu.make_async_copy(in_factor, in_w, load_sem.at[1]),
        pltpu.make_async_copy(base_weights.at[pl.ds(0, 2)], base_w, load_sem.at[2]),
        pltpu.make_async_copy(out_factors, out_w, load_sem.at[3]),
        pltpu.make_async_copy(
            gates.at[pl.ds(pl.multiple_of(me * local, local), local)], own_gates.at[me], load_sem.at[4]
        ),
        pltpu.make_async_copy(base_weights.at[2], down_w.at[me], load_sem.at[5]),
    ]
    for load in loads:
        load.start()
    pl.semaphore_wait(barrier, n * plane)

    def to_right(b, src):
        return rdma(src, all_tok.at[b], tok_r.at[b], tok_got.at[b], expert=lax.rem(me + 1, n))

    def to_left(b, src):
        return rdma(src, all_tok.at[b], tok_l.at[b], tok_got.at[b], expert=lax.rem(me + n - 1, n))

    @pl.when(me + 1 < n)
    def _():
        to_right(me, tokens).start()

    @pl.when(me >= 1)
    def _():
        to_left(me, tokens).start()

    def gate_copy(step):
        p = lax.rem(me + step, n)
        return rdma(
            gates.at[pl.ds(pl.multiple_of(p * local, local), local)], own_gates.at[me],
            gate_s.at[p], gate_r.at[me], expert=p,
        )

    for step in range(1, n):
        gate_copy(step).start()

    mine = pl.multiple_of(c * two, two)
    other = pl.multiple_of((1 - c) * two, two)

    def a_copy(b):
        return rdma(part.at[b, pl.ds(other, two)], a_got.at[b], a_s.at[b], a_r.at[b], inner=1 - c)

    def bl_copy(b):
        return rdma(
            half.at[b, :, pl.ds(0, wide)], bl_got.at[b], bl_s.at[b], bl_r.at[b], tensor=1 - x
        )

    def bb_copy(b):
        return rdma(
            half.at[b, pl.ds(pl.multiple_of((1 - x) * four, four), four), pl.ds(wide, 2 * unit)],
            bb_got.at[b], bb_s.at[b], bb_r.at[b], tensor=1 - x,
        )

    def c_copy(b):
        return rdma(lat.at[b, pl.ds(mine, two)], lat.at[b, pl.ds(mine, two)], c_s.at[b], c_r.at[b], inner=1 - c)

    quarter = c * 2 + x

    def base_copy(b, e):
        return rdma(
            piece.at[b], base_all.at[b, pl.ds(pl.multiple_of(quarter * four, four), four)],
            base_s.at[b, e], base_r.at[b, quarter], expert=e, tensor=me // 2, inner=lax.rem(me, 2),
        )

    for load in loads:
        load.wait()

    bit = unit // 2 // cuts

    def span(w, half_at):
        return pl.ds(pl.multiple_of(half_at * (unit // 2) + w * bit, bit), bit)

    def w_right(b, w, src):
        return rdma(src, down_w.at[b, span(w, y)], wr_s.at[b, w], w_got.at[b, w], expert=lax.rem(me + 1, n))

    def w_left(b, w, src):
        return rdma(src, down_w.at[b, span(w, y)], wl_s.at[b, w], w_got.at[b, w], expert=lax.rem(me + n - 1, n))

    def w_side(b, w):
        spot = down_w.at[b, span(w, y)]
        return rdma(spot, spot, wy_s.at[b, w], wy_got.at[b, w], groups=1 - y)

    def w_side_wait(b):
        for w in range(cuts):
            spot = down_w.at[b, span(w, 1 - y)]
            rdma(spot, spot, wy_s.at[b, w], wy_got.at[b, w], groups=1 - y).wait_recv()

    def w_begin():
        for w in range(cuts):
            @pl.when(me + 1 < n)
            def _():
                w_right(me, w, down_w.at[me, span(w, y)]).start()

            @pl.when(me >= 1)
            def _():
                w_left(me, w, down_w.at[me, span(w, y)]).start()

    def w_step(dist):
        for w in range(cuts):
            @pl.when(me >= dist)
            def _():
                b = lax.rem(me - dist + n, n)
                spot = down_w.at[b, span(w, y)]
                w_right(b, w, spot).wait_recv()

                @pl.when(me + 1 < n)
                def _():
                    w_right(b, w, spot).start()

                w_side(b, w).start()

            @pl.when(me + dist < n)
            def _():
                b = lax.rem(me + dist, n)
                spot = down_w.at[b, span(w, y)]
                w_left(b, w, spot).wait_recv()

                @pl.when(me >= 1)
                def _():
                    w_left(b, w, spot).start()

                w_side(b, w).start()

    def phase(k, carry):
        b = nearest(me, jnp.minimum(k, n - 1), n)

        @pl.when(k < n)
        def _():
            @pl.when(k >= 1)
            def _():
                to_right(b, all_tok.at[b]).wait_recv()

                @pl.when((b < me) & (me + 1 < n))
                def _():
                    to_right(b, all_tok.at[b]).start()

                @pl.when((b > me) & (me >= 1))
                def _():
                    to_left(b, all_tok.at[b]).start()

            t = all_tok[b]
            nt = (((1,), (1,)), ((), ()))
            value = lax.dot_general(t, in_w[...], nt, preferred_element_type=F32).astype(BF16)
            if wide > packed:
                part[b, :, packed:wide] = jnp.zeros((rows, wide - packed), BF16)
            part[b, :, 0:packed] = value
            for g in range(2):
                value = lax.dot_general(t, base_w[g], nt, preferred_element_type=F32)
                part[b, :, wide + g * unit : wide + (g + 1) * unit] = value.astype(BF16)
            a_copy(b).start()

        @pl.when((k >= 1) & (k <= n))
        def _():
            p = nearest(me, jnp.maximum(k - 1, 0), n)
            bb_copy(p).wait_recv()
            own = half[p, pl.ds(pl.multiple_of(x * four, four), four), wide : wide + 2 * unit]
            piece[p] = (own.astype(F32) + bb_got[p].astype(F32)).astype(BF16)
            for e in range(n):
                here = (me == e) & (ti == me)

                @pl.when(jnp.logical_not(here))
                def _():
                    base_copy(p, e).start()

                @pl.when(here)
                def _():
                    base_all[p, pl.ds(pl.multiple_of(quarter * four, four), four)] = piece[p]

            bl_copy(p).wait_recv()
            lat[p, pl.ds(mine, two)] = (
                half[p, :, 0:wide].astype(F32) + bl_got[p].astype(F32)
            ).astype(BF16)
            c_copy(p).start()

        @pl.when(k < n)
        def _():
            a_copy(b).wait_recv()
            half[b] = (part[b, pl.ds(mine, two)].astype(F32) + a_got[b].astype(F32)).astype(BF16)
            bb_copy(b).start()
            bl_copy(b).start()

        @pl.when(k >= 2)
        def _():
            p = nearest(me, jnp.maximum(k - 2, 0), n)
            rdma(
                lat.at[p, pl.ds(other, two)], lat.at[p, pl.ds(other, two)], c_s.at[p], c_r.at[p],
                inner=1 - c,
            ).wait_recv()
            value = lat[p, :, 0:packed]
            for j in range(local):
                own = value * mask[j : j + 1, :].astype(BF16)
                for g in range(2):
                    delta[p, j, :, g * hid : (g + 1) * hid] = jnp.dot(
                        own, out_w[g], preferred_element_type=F32
                    ).astype(BF16)

        return carry

    lax.fori_loop(0, n + 2, phase, 0)
    w_begin()

    for step in range(1, n):
        p = lax.rem(me + step, n)
        rdma(own_gates.at[p], own_gates.at[p], gate_s.at[p], gate_r.at[p], expert=p).wait_recv()

    def comb_copy(b):
        return rdma(comb.at[b], comb_got.at[me], comb_s.at[b], comb_r.at[me], expert=b)

    def finish(k, carry):
        b = nearest(ti, k, n)
        for q in range(plane):
            @pl.when(jnp.logical_not((me == ti) & (quarter == q)))
            def _():
                spot = base_all.at[b, pl.ds(q * four, four)]
                rdma(spot, spot, base_s.at[b, 0], base_r.at[b, q], tensor=1 - x).wait_recv()

        pick = (
            lax.broadcasted_iota(jnp.int32, (local, 128), 0)
            == lax.broadcasted_iota(jnp.int32, (local, 128), 1)
        ).astype(F32)
        weight = lax.dot_general(
            own_gates[b], pick, (((0,), (0,)), ((), ())),
            preferred_element_type=F32, precision=lax.Precision.HIGHEST,
        )
        gate_base = base_all[b, :, 0:unit].astype(F32)
        up_base = base_all[b, :, unit : 2 * unit].astype(F32)
        total = jnp.zeros((rows, hid), F32)
        for j in range(local):
            v = gate_base + delta[b, j, :, 0:hid].astype(F32)
            u = up_base + delta[b, j, :, hid : 2 * hid].astype(F32)
            total = total + weight[:, j : j + 1] * (v / (1.0 + jnp.exp(-v)) * u)
        comb[b] = total.astype(BF16)

        @pl.when(b != me)
        def _():
            comb_copy(b).start()

        return carry

    lax.fori_loop(0, n - 1, finish, 0)
    w_step(1)
    finish(n - 1, 0)

    total = comb[me].astype(F32)
    for step in range(1, n):
        p = lax.rem(me + step, n)
        rdma(comb_got.at[p], comb_got.at[p], comb_s.at[p], comb_r.at[p], expert=p).wait_recv()
        total = total + comb_got[p].astype(F32)
    full[ti] = total.astype(BF16)

    def ag_copy(step):
        to = lax.rem(ti + step, plane)
        return rdma(
            full.at[ti], full.at[ti], ag_s.at[to], ag_r.at[ti], tensor=to // 2, inner=lax.rem(to, 2)
        )

    for step in range(1, plane):
        ag_copy(step).start()
    for dist in range(2, n - 1):
        w_step(dist)
    for step in range(1, plane):
        p = lax.rem(ti + step, plane)
        rdma(full.at[p], full.at[p], ag_s.at[p], ag_r.at[p], tensor=1 - x).wait_recv()
    acc[...] = jnp.dot(full[me], down_w[me], preferred_element_type=F32)
    if n > 2:
        w_step(n - 1)
    for k in range(1, n):
        b = nearest(me, k, n)
        w_side_wait(b)
        acc[...] += jnp.dot(full[b], down_w[b], preferred_element_type=F32)
    out[...] = acc[...].astype(BF16)

    for b in range(n):
        @pl.when((b <= me) & (me + 1 < n))
        def _():
            to_right(b, all_tok.at[b]).wait_send()

        @pl.when((b >= me) & (me >= 1))
        def _():
            to_left(b, all_tok.at[b]).wait_send()

        a_copy(b).wait_send()
        bl_copy(b).wait_send()
        bb_copy(b).wait_send()
        c_copy(b).wait_send()
        for e in range(n):
            @pl.when(jnp.logical_not((me == e) & (ti == me)))
            def _():
                base_copy(b, e).wait_send()

        @pl.when(b != me)
        def _():
            comb_copy(b).wait_send()
            for w in range(cuts):
                w_side(b, w).wait_send()

        for w in range(cuts):
            @pl.when((b <= me) & (me + 1 < n))
            def _():
                w_right(b, w, down_w.at[b, span(w, y)]).wait_send()

            @pl.when((b >= me) & (me >= 1))
            def _():
                w_left(b, w, down_w.at[b, span(w, y)]).wait_send()

    for step in range(1, n):
        gate_copy(step).wait_send()
    for step in range(1, plane):
        ag_copy(step).wait_send()


def layer(tokens, dense_gates, base_weights, in_factor, out_factors, ranks):
    rows, feat = tokens.shape
    n = lax.axis_size("expert")
    plane = lax.axis_size("tensor") * lax.axis_size("inner")
    local = ranks.shape[0]
    packed = in_factor.shape[0]
    wide = -(-packed // 128) * 128
    unit = base_weights.shape[1]
    hid = out_factors.shape[2]
    order = lax.broadcasted_iota(jnp.int32, (local, local), 0)
    other = lax.broadcasted_iota(jnp.int32, (local, local), 1)
    ends = jnp.sum(jnp.where(other <= order, ranks[None, :], 0), axis=1)[:, None]
    place = lax.broadcasted_iota(jnp.int32, (local, packed), 1)
    mask = ((place < ends) & (place >= ends - ranks[:, None])).astype(F32)
    two, four = rows // 2, rows // 4
    cuts = 2
    vmem = pltpu.VMEM
    dma = pltpu.SemaphoreType.DMA
    return pl.pallas_call(
        functools.partial(fused, n, plane),
        out_shape=jax.ShapeDtypeStruct((rows, feat), BF16),
        in_specs=[
            pl.BlockSpec(memory_space=pl.ANY),
            pl.BlockSpec(memory_space=vmem),
            pl.BlockSpec(memory_space=vmem),
            pl.BlockSpec(memory_space=pl.ANY),
            pl.BlockSpec(memory_space=pl.ANY),
            pl.BlockSpec(memory_space=pl.ANY),
        ],
        out_specs=pl.BlockSpec(memory_space=vmem),
        scratch_shapes=[
            vmem((n, rows, feat), BF16),
            vmem((2, unit, feat), BF16),
            vmem((packed, feat), BF16),
            vmem((2, packed, hid), BF16),
            vmem((n, local, rows), F32),
            vmem((n, rows, wide + 2 * unit), BF16),
            vmem((n, two, wide + 2 * unit), BF16),
            vmem((n, two, wide + 2 * unit), BF16),
            vmem((n, two, wide), BF16),
            vmem((n, four, 2 * unit), BF16),
            vmem((n, rows, wide), BF16),
            vmem((n, four, 2 * unit), BF16),
            vmem((n, rows, 2 * unit), BF16),
            vmem((n, local, rows, 2 * hid), BF16),
            vmem((n, rows, hid), BF16),
            vmem((n, rows, hid), BF16),
            vmem((plane, rows, hid), BF16),
            vmem((n, unit, feat), BF16),
            vmem((rows, feat), F32),
            dma((6,)),
            dma((n,)), dma((n,)), dma((n,)), dma((n,)), dma((n,)),
            dma((n,)), dma((n,)), dma((n,)), dma((n,)), dma((n,)), dma((n,)), dma((n,)), dma((n,)),
            dma((n, n)), dma((n, plane)), dma((n,)), dma((n,)), dma((plane,)), dma((plane,)),
            dma((n, cuts)), dma((n, cuts)), dma((n, cuts)), dma((n, cuts)), dma((n, cuts)),
        ],
        compiler_params=pltpu.CompilerParams(
            collective_id=0, has_side_effects=True, vmem_limit_bytes=60 * 1024 * 1024
        ),
        cost_estimate=pl.CostEstimate(
            flops=60_000_000_000, bytes_accessed=20_000_000, transcendentals=0
        ),
    )(tokens, dense_gates.T, mask, base_weights, in_factor, out_factors)


def on_device(tokens, expert_ids, gate_weights, base_weights, in_factor, out_factors, ranks):
    tok_rows, feat_slice = tokens.shape
    owners = lax.axis_size("expert")
    local_count = ranks.shape[0]
    experts = local_count * owners
    packed = in_factor.shape[0]
    hidden_rows = base_weights.shape[1]
    hidden_slice = out_factors.shape[2]
    rows = tok_rows * owners

    columns = lax.broadcasted_iota(jnp.int32, (1, 1, experts), 2)
    chosen = expert_ids[:, :, None] == columns
    dense_gates = jnp.sum(jnp.where(chosen, gate_weights[:, :, None], 0.0), axis=1)
    tensor, inner = lax.axis_size("tensor"), lax.axis_size("inner")
    square = tensor == 2 and inner == 2 and owners == tensor * inner
    if square and lax.axis_size("groups") == 2 and tok_rows % 64 == 0 and hidden_rows % 64 == 0:
        return layer(tokens, dense_gates, base_weights, in_factor, out_factors, ranks)
    down = lax.all_gather(base_weights[2], "expert", axis=0, tiled=True)
    all_tokens = lax.all_gather(tokens, "expert", axis=0, tiled=True)
    all_gates = lax.all_gather(dense_gates, "expert", axis=0, tiled=True)
    own_gates = lax.dynamic_slice_in_dim(
        all_gates, lax.axis_index("expert") * local_count, local_count, 1
    )

    latent_part = lax.dot_general(
        all_tokens, in_factor, (((1,), (1,)), ((), ())), preferred_element_type=jnp.float32
    ).astype(jnp.bfloat16)
    latent = lax.psum(latent_part, FEATURE_AXES)

    base_part = lax.dot_general(
        all_tokens,
        base_weights[:2].reshape(2 * hidden_rows, feat_slice),
        (((1,), (1,)), ((), ())),
        preferred_element_type=jnp.float32,
    ).astype(jnp.bfloat16)
    base = lax.psum_scatter(base_part, FEATURE_AXES, scatter_dimension=0, tiled=True)
    base = base.reshape(-1, 2, hidden_rows)
    base = lax.all_gather(base, "expert", axis=2, tiled=True)
    base = lax.all_to_all(base, FEATURE_AXES, split_axis=2, concat_axis=0, tiled=True)
    gate_rows = base[:, 0].astype(jnp.float32)
    up_rows = base[:, 1].astype(jnp.float32)

    order = lax.broadcasted_iota(jnp.int32, (local_count, local_count), 0)
    other = lax.broadcasted_iota(jnp.int32, (local_count, local_count), 1)
    ends = jnp.sum(jnp.where(other <= order, ranks[None, :], 0), axis=1)
    where = lax.broadcasted_iota(jnp.int32, (1, packed), 1)
    combined = jnp.zeros((rows, hidden_slice), jnp.float32)
    for member in range(local_count):
        inside = (where >= ends[member] - ranks[member]) & (where < ends[member])
        own = jnp.where(inside, latent, jnp.zeros((), jnp.bfloat16))
        gate = jnp.dot(own, out_factors[0], preferred_element_type=jnp.float32)
        up = jnp.dot(own, out_factors[1], preferred_element_type=jnp.float32)
        hidden = jax.nn.silu(gate_rows + gate) * (up_rows + up)
        combined = combined + own_gates[:, member : member + 1] * hidden
    combined = lax.psum_scatter(
        combined.astype(jnp.bfloat16), "expert", scatter_dimension=0, tiled=True
    )
    full_hidden = lax.all_gather(combined, FEATURE_AXES, axis=1, tiled=True)
    return jnp.dot(full_hidden, down, preferred_element_type=jnp.float32).astype(jnp.bfloat16)


def solution(mesh):
    return jax.shard_map(
        on_device,
        mesh=mesh,
        in_specs=(
            P(("groups", "expert"), ("tensor", "inner")),
            P(("groups", "expert"), None),
            P(("groups", "expert"), None),
            P(None, "expert", ("tensor", "inner")),
            P("expert", ("tensor", "inner")),
            P(None, "expert", ("tensor", "inner")),
            P("expert"),
        ),
        out_specs=P(("groups", "expert"), ("tensor", "inner")),
        check_vma=False,
    )
```

```python
import functools
import jax
import jax.numpy as jnp
from jax import lax
from jax.experimental import pallas as pl
from jax.experimental.pallas import tpu as pltpu
from jax.sharding import PartitionSpec as P

FEATURE_AXES = ("tensor", "inner")
MESH = pl.DeviceIdType.MESH
BF16 = jnp.bfloat16
F32 = jnp.float32


def nearest(at, k, n):
    both = jnp.minimum(at, n - 1 - at)
    near = (k + 1) // 2
    left_near = k % 2
    far = k - both
    left_far = (at > n - 1 - at).astype(jnp.int32)
    inside = (k <= 2 * both).astype(jnp.int32)
    dist = inside * near + (1 - inside) * far
    left = inside * left_near + (1 - inside) * left_far
    return at + dist * (1 - 2 * left)


def fused(
    n, plane, tokens, gates, mask, base_weights, in_factor, out_factors, out,
    all_tok, base_w, in_w, out_w, own_gates, part, a_got, half, bl_got, bb_got, lat, piece,
    base_all, delta, comb, comb_got, full, down_w, acc,
    load_sem, tok_l, tok_r, tok_got, gate_s, gate_r, a_s, a_r, bl_s, bl_r, bb_s, bb_r, c_s, c_r,
    base_s, base_r, comb_s, comb_r, ag_s, ag_r, wl_s, wr_s, w_got, wy_s, wy_got,
):
    me = lax.axis_index("expert")
    x = lax.axis_index("tensor")
    c = lax.axis_index("inner")
    y = lax.axis_index("groups")
    ti = x * 2 + c
    cuts = w_got.shape[1]
    rows = tokens.shape[0]
    packed = in_factor.shape[0]
    wide = bl_got.shape[2]
    unit = base_weights.shape[1]
    local = mask.shape[0]
    hid = out_factors.shape[2]
    two, four = rows // 2, rows // 4

    def rdma(src, dst, send, recv, **where):
        return pltpu.make_async_remote_copy(
            src_ref=src, dst_ref=dst, send_sem=send, recv_sem=recv,
            device_id=where, device_id_type=MESH,
        )

    barrier = pltpu.get_barrier_semaphore()
    for de in range(n):
        for dt in range(plane):
            if de or dt:
                to = lax.rem(ti + dt, plane)
                pl.semaphore_signal(
                    barrier, inc=1,
                    device_id={"expert": lax.rem(me + de, n), "tensor": to // 2, "inner": lax.rem(to, 2)},
                    device_id_type=MESH,
                )
    pl.semaphore_signal(barrier, inc=1, device_id={"groups": 1 - y}, device_id_type=MESH)
    loads = [
        pltpu.make_async_copy(tokens, all_tok.at[me], load_sem.at[0]),
        pltpu.make_async_copy(in_factor, in_w, load_sem.at[1]),
        pltpu.make_async_copy(base_weights.at[pl.ds(0, 2)], base_w, load_sem.at[2]),
        pltpu.make_async_copy(out_factors, out_w, load_sem.at[3]),
        pltpu.make_async_copy(
            gates.at[pl.ds(pl.multiple_of(me * local, local), local)], own_gates.at[me], load_sem.at[4]
        ),
        pltpu.make_async_copy(base_weights.at[2], down_w.at[me], load_sem.at[5]),
    ]
    for load in loads:
        load.start()
    pl.semaphore_wait(barrier, n * plane)

    def to_right(b, src):
        return rdma(src, all_tok.at[b], tok_r.at[b], tok_got.at[b], expert=lax.rem(me + 1, n))

    def to_left(b, src):
        return rdma(src, all_tok.at[b], tok_l.at[b], tok_got.at[b], expert=lax.rem(me + n - 1, n))

    @pl.when(me + 1 < n)
    def _():
        to_right(me, tokens).start()

    @pl.when(me >= 1)
    def _():
        to_left(me, tokens).start()

    def gate_copy(step):
        p = lax.rem(me + step, n)
        return rdma(
            gates.at[pl.ds(pl.multiple_of(p * local, local), local)], own_gates.at[me],
            gate_s.at[p], gate_r.at[me], expert=p,
        )

    for step in range(1, n):
        gate_copy(step).start()

    mine = pl.multiple_of(c * two, two)
    other = pl.multiple_of((1 - c) * two, two)

    def a_copy(b):
        return rdma(part.at[b, pl.ds(other, two)], a_got.at[b], a_s.at[b], a_r.at[b], inner=1 - c)

    def bl_copy(b):
        return rdma(
            half.at[b, :, pl.ds(0, wide)], bl_got.at[b], bl_s.at[b], bl_r.at[b], tensor=1 - x
        )

    def bb_copy(b):
        return rdma(
            half.at[b, pl.ds(pl.multiple_of((1 - x) * four, four), four), pl.ds(wide, 2 * unit)],
            bb_got.at[b], bb_s.at[b], bb_r.at[b], tensor=1 - x,
        )

    def c_copy(b):
        return rdma(lat.at[b, pl.ds(mine, two)], lat.at[b, pl.ds(mine, two)], c_s.at[b], c_r.at[b], inner=1 - c)

    quarter = c * 2 + x

    def base_copy(b, e):
        return rdma(
            piece.at[b], base_all.at[b, pl.ds(pl.multiple_of(quarter * four, four), four)],
            base_s.at[b, e], base_r.at[b, quarter], expert=e, tensor=me // 2, inner=lax.rem(me, 2),
        )

    for load in loads:
        load.wait()

    bit = unit // 2 // cuts

    def span(w, half_at):
        return pl.ds(pl.multiple_of(half_at * (unit // 2) + w * bit, bit), bit)

    def w_right(b, w, src):
        return rdma(src, down_w.at[b, span(w, y)], wr_s.at[b, w], w_got.at[b, w], expert=lax.rem(me + 1, n))

    def w_left(b, w, src):
        return rdma(src, down_w.at[b, span(w, y)], wl_s.at[b, w], w_got.at[b, w], expert=lax.rem(me + n - 1, n))

    def w_side(b, w):
        spot = down_w.at[b, span(w, y)]
        return rdma(spot, spot, wy_s.at[b, w], wy_got.at[b, w], groups=1 - y)

    def w_side_wait(b):
        for w in range(cuts):
            spot = down_w.at[b, span(w, 1 - y)]
            rdma(spot, spot, wy_s.at[b, w], wy_got.at[b, w], groups=1 - y).wait_recv()

    def reach(k):
        d = nearest(me, jnp.minimum(k, n - 1), n) - me
        return jnp.where(k >= n, n, jnp.maximum(d, -d))

    def w_begin(k):
        now, before = reach(k), reach(jnp.maximum(k - 1, 0))

        @pl.when((me + 1 < n) & (now >= me + 1) & (before < me + 1))
        def _():
            for w in range(cuts):
                w_right(me, w, down_w.at[me, span(w, y)]).start()

        @pl.when((me >= 1) & (now >= n - me) & (before < n - me))
        def _():
            for w in range(cuts):
                w_left(me, w, down_w.at[me, span(w, y)]).start()

    def w_step(dist):
        for w in range(cuts):
            @pl.when(me >= dist)
            def _():
                b = lax.rem(me - dist + n, n)
                spot = down_w.at[b, span(w, y)]
                w_right(b, w, spot).wait_recv()

                @pl.when(me + 1 < n)
                def _():
                    w_right(b, w, spot).start()

                w_side(b, w).start()

            @pl.when(me + dist < n)
            def _():
                b = lax.rem(me + dist, n)
                spot = down_w.at[b, span(w, y)]
                w_left(b, w, spot).wait_recv()

                @pl.when(me >= 1)
                def _():
                    w_left(b, w, spot).start()

                w_side(b, w).start()

    def phase(k, carry):
        b = nearest(me, jnp.minimum(k, n - 1), n)

        @pl.when(k < n)
        def _():
            @pl.when(k >= 1)
            def _():
                to_right(b, all_tok.at[b]).wait_recv()

                @pl.when((b < me) & (me + 1 < n))
                def _():
                    to_right(b, all_tok.at[b]).start()

                @pl.when((b > me) & (me >= 1))
                def _():
                    to_left(b, all_tok.at[b]).start()

            w_begin(k)
            t = all_tok[b]
            nt = (((1,), (1,)), ((), ()))
            value = lax.dot_general(t, in_w[...], nt, preferred_element_type=F32).astype(BF16)
            if wide > packed:
                part[b, :, packed:wide] = jnp.zeros((rows, wide - packed), BF16)
            part[b, :, 0:packed] = value
            for g in range(2):
                value = lax.dot_general(t, base_w[g], nt, preferred_element_type=F32)
                part[b, :, wide + g * unit : wide + (g + 1) * unit] = value.astype(BF16)
            a_copy(b).start()

        @pl.when(k == n)
        def _():
            w_begin(n)

        @pl.when(k == n + 1)
        def _():
            w_step(1)

        @pl.when((k >= 1) & (k <= n))
        def _():
            p = nearest(me, jnp.maximum(k - 1, 0), n)
            bb_copy(p).wait_recv()
            own = half[p, pl.ds(pl.multiple_of(x * four, four), four), wide : wide + 2 * unit]
            piece[p] = (own.astype(F32) + bb_got[p].astype(F32)).astype(BF16)
            for e in range(n):
                here = (me == e) & (ti == me)

                @pl.when(jnp.logical_not(here))
                def _():
                    base_copy(p, e).start()

                @pl.when(here)
                def _():
                    base_all[p, pl.ds(pl.multiple_of(quarter * four, four), four)] = piece[p]

            bl_copy(p).wait_recv()
            lat[p, pl.ds(mine, two)] = (
                half[p, :, 0:wide].astype(F32) + bl_got[p].astype(F32)
            ).astype(BF16)
            c_copy(p).start()

        @pl.when(k < n)
        def _():
            a_copy(b).wait_recv()
            half[b] = (part[b, pl.ds(mine, two)].astype(F32) + a_got[b].astype(F32)).astype(BF16)
            bb_copy(b).start()
            bl_copy(b).start()

        @pl.when(k >= 2)
        def _():
            p = nearest(me, jnp.maximum(k - 2, 0), n)
            rdma(
                lat.at[p, pl.ds(other, two)], lat.at[p, pl.ds(other, two)], c_s.at[p], c_r.at[p],
                inner=1 - c,
            ).wait_recv()
            value = lat[p, :, 0:packed]
            for j in range(local):
                own = value * mask[j : j + 1, :].astype(BF16)
                for g in range(2):
                    delta[p, j, :, g * hid : (g + 1) * hid] = jnp.dot(
                        own, out_w[g], preferred_element_type=F32
                    ).astype(BF16)

        return carry

    lax.fori_loop(0, n + 2, phase, 0)

    for step in range(1, n):
        p = lax.rem(me + step, n)
        rdma(own_gates.at[p], own_gates.at[p], gate_s.at[p], gate_r.at[p], expert=p).wait_recv()

    def comb_copy(b):
        return rdma(comb.at[b], comb_got.at[me], comb_s.at[b], comb_r.at[me], expert=b)

    def finish(k, carry):
        b = nearest(ti, k, n)
        for q in range(plane):
            @pl.when(jnp.logical_not((me == ti) & (quarter == q)))
            def _():
                spot = base_all.at[b, pl.ds(q * four, four)]
                rdma(spot, spot, base_s.at[b, 0], base_r.at[b, q], tensor=1 - x).wait_recv()

        pick = (
            lax.broadcasted_iota(jnp.int32, (local, 128), 0)
            == lax.broadcasted_iota(jnp.int32, (local, 128), 1)
        ).astype(F32)
        weight = lax.dot_general(
            own_gates[b], pick, (((0,), (0,)), ((), ())),
            preferred_element_type=F32, precision=lax.Precision.HIGHEST,
        )
        gate_base = base_all[b, :, 0:unit].astype(F32)
        up_base = base_all[b, :, unit : 2 * unit].astype(F32)
        total = jnp.zeros((rows, hid), F32)
        for j in range(local):
            v = gate_base + delta[b, j, :, 0:hid].astype(F32)
            u = up_base + delta[b, j, :, hid : 2 * hid].astype(F32)
            total = total + weight[:, j : j + 1] * (v * (0.5 + 0.5 * jnp.tanh(0.5 * v)) * u)
        comb[b] = total.astype(BF16)

        @pl.when(b != me)
        def _():
            comb_copy(b).start()

        return carry

    lax.fori_loop(0, n - 1, finish, 0)
    for dist in range(2, n - 1):
        w_step(dist)
    finish(n - 1, 0)

    total = comb[me].astype(F32)
    for step in range(1, n):
        p = lax.rem(me + step, n)
        rdma(comb_got.at[p], comb_got.at[p], comb_s.at[p], comb_r.at[p], expert=p).wait_recv()
        total = total + comb_got[p].astype(F32)
    full[ti] = total.astype(BF16)

    def ag_copy(step):
        to = lax.rem(ti + step, plane)
        return rdma(
            full.at[ti], full.at[ti], ag_s.at[to], ag_r.at[ti], tensor=to // 2, inner=lax.rem(to, 2)
        )

    for step in range(1, plane):
        ag_copy(step).start()
    for step in range(1, plane):
        p = lax.rem(ti + step, plane)
        rdma(full.at[p], full.at[p], ag_s.at[p], ag_r.at[p], tensor=1 - x).wait_recv()
    acc[...] = jnp.dot(full[me], down_w[me], preferred_element_type=F32)
    if n > 2:
        w_step(n - 1)
    for k in range(1, n):
        b = nearest(me, k, n)
        w_side_wait(b)
        acc[...] += jnp.dot(full[b], down_w[b], preferred_element_type=F32)
    out[...] = acc[...].astype(BF16)

    for b in range(n):
        @pl.when((b <= me) & (me + 1 < n))
        def _():
            to_right(b, all_tok.at[b]).wait_send()

        @pl.when((b >= me) & (me >= 1))
        def _():
            to_left(b, all_tok.at[b]).wait_send()

        a_copy(b).wait_send()
        bl_copy(b).wait_send()
        bb_copy(b).wait_send()
        c_copy(b).wait_send()
        for e in range(n):
            @pl.when(jnp.logical_not((me == e) & (ti == me)))
            def _():
                base_copy(b, e).wait_send()

        @pl.when(b != me)
        def _():
            comb_copy(b).wait_send()
            for w in range(cuts):
                w_side(b, w).wait_send()

        for w in range(cuts):
            @pl.when((b <= me) & (me + 1 < n))
            def _():
                w_right(b, w, down_w.at[b, span(w, y)]).wait_send()

            @pl.when((b >= me) & (me >= 1))
            def _():
                w_left(b, w, down_w.at[b, span(w, y)]).wait_send()

    for step in range(1, n):
        gate_copy(step).wait_send()
    for step in range(1, plane):
        ag_copy(step).wait_send()


def layer(tokens, dense_gates, base_weights, in_factor, out_factors, ranks):
    rows, feat = tokens.shape
    n = lax.axis_size("expert")
    plane = lax.axis_size("tensor") * lax.axis_size("inner")
    local = ranks.shape[0]
    packed = in_factor.shape[0]
    wide = -(-packed // 128) * 128
    unit = base_weights.shape[1]
    hid = out_factors.shape[2]
    order = lax.broadcasted_iota(jnp.int32, (local, local), 0)
    other = lax.broadcasted_iota(jnp.int32, (local, local), 1)
    ends = jnp.sum(jnp.where(other <= order, ranks[None, :], 0), axis=1)[:, None]
    place = lax.broadcasted_iota(jnp.int32, (local, packed), 1)
    mask = ((place < ends) & (place >= ends - ranks[:, None])).astype(F32)
    two, four = rows // 2, rows // 4
    cuts = 2
    vmem = pltpu.VMEM
    dma = pltpu.SemaphoreType.DMA
    return pl.pallas_call(
        functools.partial(fused, n, plane),
        out_shape=jax.ShapeDtypeStruct((rows, feat), BF16),
        in_specs=[
            pl.BlockSpec(memory_space=pl.ANY),
            pl.BlockSpec(memory_space=vmem),
            pl.BlockSpec(memory_space=vmem),
            pl.BlockSpec(memory_space=pl.ANY),
            pl.BlockSpec(memory_space=pl.ANY),
            pl.BlockSpec(memory_space=pl.ANY),
        ],
        out_specs=pl.BlockSpec(memory_space=vmem),
        scratch_shapes=[
            vmem((n, rows, feat), BF16),
            vmem((2, unit, feat), BF16),
            vmem((packed, feat), BF16),
            vmem((2, packed, hid), BF16),
            vmem((n, local, rows), F32),
            vmem((n, rows, wide + 2 * unit), BF16),
            vmem((n, two, wide + 2 * unit), BF16),
            vmem((n, two, wide + 2 * unit), BF16),
            vmem((n, two, wide), BF16),
            vmem((n, four, 2 * unit), BF16),
            vmem((n, rows, wide), BF16),
            vmem((n, four, 2 * unit), BF16),
            vmem((n, rows, 2 * unit), BF16),
            vmem((n, local, rows, 2 * hid), BF16),
            vmem((n, rows, hid), BF16),
            vmem((n, rows, hid), BF16),
            vmem((plane, rows, hid), BF16),
            vmem((n, unit, feat), BF16),
            vmem((rows, feat), F32),
            dma((6,)),
            dma((n,)), dma((n,)), dma((n,)), dma((n,)), dma((n,)),
            dma((n,)), dma((n,)), dma((n,)), dma((n,)), dma((n,)), dma((n,)), dma((n,)), dma((n,)),
            dma((n, n)), dma((n, plane)), dma((n,)), dma((n,)), dma((plane,)), dma((plane,)),
            dma((n, cuts)), dma((n, cuts)), dma((n, cuts)), dma((n, cuts)), dma((n, cuts)),
        ],
        compiler_params=pltpu.CompilerParams(
            collective_id=0, has_side_effects=True, vmem_limit_bytes=60 * 1024 * 1024
        ),
        cost_estimate=pl.CostEstimate(
            flops=60_000_000_000, bytes_accessed=20_000_000, transcendentals=0
        ),
    )(tokens, dense_gates.T, mask, base_weights, in_factor, out_factors)


def on_device(tokens, expert_ids, gate_weights, base_weights, in_factor, out_factors, ranks):
    tok_rows, feat_slice = tokens.shape
    owners = lax.axis_size("expert")
    local_count = ranks.shape[0]
    experts = local_count * owners
    packed = in_factor.shape[0]
    hidden_rows = base_weights.shape[1]
    hidden_slice = out_factors.shape[2]
    rows = tok_rows * owners

    columns = lax.broadcasted_iota(jnp.int32, (1, 1, experts), 2)
    chosen = expert_ids[:, :, None] == columns
    dense_gates = jnp.sum(jnp.where(chosen, gate_weights[:, :, None], 0.0), axis=1)
    tensor, inner = lax.axis_size("tensor"), lax.axis_size("inner")
    square = tensor == 2 and inner == 2 and owners == tensor * inner
    if square and lax.axis_size("groups") == 2 and tok_rows % 64 == 0 and hidden_rows % 64 == 0:
        return layer(tokens, dense_gates, base_weights, in_factor, out_factors, ranks)
    down = lax.all_gather(base_weights[2], "expert", axis=0, tiled=True)
    all_tokens = lax.all_gather(tokens, "expert", axis=0, tiled=True)
    all_gates = lax.all_gather(dense_gates, "expert", axis=0, tiled=True)
    own_gates = lax.dynamic_slice_in_dim(
        all_gates, lax.axis_index("expert") * local_count, local_count, 1
    )

    latent_part = lax.dot_general(
        all_tokens, in_factor, (((1,), (1,)), ((), ())), preferred_element_type=jnp.float32
    ).astype(jnp.bfloat16)
    latent = lax.psum(latent_part, FEATURE_AXES)

    base_part = lax.dot_general(
        all_tokens,
        base_weights[:2].reshape(2 * hidden_rows, feat_slice),
        (((1,), (1,)), ((), ())),
        preferred_element_type=jnp.float32,
    ).astype(jnp.bfloat16)
    base = lax.psum_scatter(base_part, FEATURE_AXES, scatter_dimension=0, tiled=True)
    base = base.reshape(-1, 2, hidden_rows)
    base = lax.all_gather(base, "expert", axis=2, tiled=True)
    base = lax.all_to_all(base, FEATURE_AXES, split_axis=2, concat_axis=0, tiled=True)
    gate_rows = base[:, 0].astype(jnp.float32)
    up_rows = base[:, 1].astype(jnp.float32)

    order = lax.broadcasted_iota(jnp.int32, (local_count, local_count), 0)
    other = lax.broadcasted_iota(jnp.int32, (local_count, local_count), 1)
    ends = jnp.sum(jnp.where(other <= order, ranks[None, :], 0), axis=1)
    where = lax.broadcasted_iota(jnp.int32, (1, packed), 1)
    combined = jnp.zeros((rows, hidden_slice), jnp.float32)
    for member in range(local_count):
        inside = (where >= ends[member] - ranks[member]) & (where < ends[member])
        own = jnp.where(inside, latent, jnp.zeros((), jnp.bfloat16))
        gate = jnp.dot(own, out_factors[0], preferred_element_type=jnp.float32)
        up = jnp.dot(own, out_factors[1], preferred_element_type=jnp.float32)
        hidden = jax.nn.silu(gate_rows + gate) * (up_rows + up)
        combined = combined + own_gates[:, member : member + 1] * hidden
    combined = lax.psum_scatter(
        combined.astype(jnp.bfloat16), "expert", scatter_dimension=0, tiled=True
    )
    full_hidden = lax.all_gather(combined, FEATURE_AXES, axis=1, tiled=True)
    return jnp.dot(full_hidden, down, preferred_element_type=jnp.float32).astype(jnp.bfloat16)


def solution(mesh):
    return jax.shard_map(
        on_device,
        mesh=mesh,
        in_specs=(
            P(("groups", "expert"), ("tensor", "inner")),
            P(("groups", "expert"), None),
            P(("groups", "expert"), None),
            P(None, "expert", ("tensor", "inner")),
            P("expert", ("tensor", "inner")),
            P(None, "expert", ("tensor", "inner")),
            P("expert"),
        ),
        out_specs=P(("groups", "expert"), ("tensor", "inner")),
        check_vma=False,
    )
```

```python
import functools
import jax
import jax.numpy as jnp
from jax import lax
from jax.experimental import pallas as pl
from jax.experimental.pallas import tpu as pltpu
from jax.sharding import PartitionSpec as P

FEATURE_AXES = ("tensor", "inner")
MESH = pl.DeviceIdType.MESH
BF16 = jnp.bfloat16
F32 = jnp.float32


def nearest(at, k, n):
    both = jnp.minimum(at, n - 1 - at)
    near = (k + 1) // 2
    left_near = k % 2
    far = k - both
    left_far = (at > n - 1 - at).astype(jnp.int32)
    inside = (k <= 2 * both).astype(jnp.int32)
    dist = inside * near + (1 - inside) * far
    left = inside * left_near + (1 - inside) * left_far
    return at + dist * (1 - 2 * left)


def fused(
    n, plane, tokens, gates, mask, base_weights, in_factor, out_factors, out,
    all_tok, base_w, in_w, out_w, own_gates, part, a_got, half, bl_got, bb_got, lat, piece,
    base_all, delta, comb, comb_got, full, down_w, acc,
    load_sem, tok_l, tok_r, tok_got, gate_s, gate_r, a_s, a_r, bl_s, bl_r, bb_s, bb_r, c_s, c_r,
    base_s, base_r, comb_s, comb_r, ag_s, ag_r, wl_s, wr_s, w_got, wy_s, wy_got,
):
    me = lax.axis_index("expert")
    x = lax.axis_index("tensor")
    c = lax.axis_index("inner")
    y = lax.axis_index("groups")
    ti = x * 2 + c
    cuts = w_got.shape[1]
    rows = tokens.shape[0]
    packed = in_factor.shape[0]
    wide = bl_got.shape[2]
    unit = base_weights.shape[1]
    local = mask.shape[0]
    hid = out_factors.shape[2]
    two, four = rows // 2, rows // 4

    def rdma(src, dst, send, recv, **where):
        return pltpu.make_async_remote_copy(
            src_ref=src, dst_ref=dst, send_sem=send, recv_sem=recv,
            device_id=where, device_id_type=MESH,
        )

    barrier = pltpu.get_barrier_semaphore()
    for de in range(n):
        for dt in range(plane):
            if de or dt:
                to = lax.rem(ti + dt, plane)
                pl.semaphore_signal(
                    barrier, inc=1,
                    device_id={"expert": lax.rem(me + de, n), "tensor": to // 2, "inner": lax.rem(to, 2)},
                    device_id_type=MESH,
                )
    pl.semaphore_signal(barrier, inc=1, device_id={"groups": 1 - y}, device_id_type=MESH)
    loads = [
        pltpu.make_async_copy(tokens, all_tok.at[me], load_sem.at[0]),
        pltpu.make_async_copy(in_factor, in_w, load_sem.at[1]),
        pltpu.make_async_copy(base_weights.at[pl.ds(0, 2)], base_w, load_sem.at[2]),
        pltpu.make_async_copy(out_factors, out_w, load_sem.at[3]),
        pltpu.make_async_copy(
            gates.at[pl.ds(pl.multiple_of(me * local, local), local)], own_gates.at[me], load_sem.at[4]
        ),
        pltpu.make_async_copy(base_weights.at[2], down_w.at[me], load_sem.at[5]),
    ]
    for load in loads:
        load.start()
    pl.semaphore_wait(barrier, n * plane)

    def to_right(b, src):
        return rdma(src, all_tok.at[b], tok_r.at[b], tok_got.at[b], expert=lax.rem(me + 1, n))

    def to_left(b, src):
        return rdma(src, all_tok.at[b], tok_l.at[b], tok_got.at[b], expert=lax.rem(me + n - 1, n))

    @pl.when(me + 1 < n)
    def _():
        to_right(me, tokens).start()

    @pl.when(me >= 1)
    def _():
        to_left(me, tokens).start()

    def gate_copy(step):
        p = lax.rem(me + step, n)
        return rdma(
            gates.at[pl.ds(pl.multiple_of(p * local, local), local)], own_gates.at[me],
            gate_s.at[p], gate_r.at[me], expert=p,
        )

    for step in range(1, n):
        gate_copy(step).start()

    mine = pl.multiple_of(c * two, two)
    other = pl.multiple_of((1 - c) * two, two)

    def a_copy(b):
        return rdma(part.at[b, pl.ds(other, two)], a_got.at[b], a_s.at[b], a_r.at[b], inner=1 - c)

    def bl_copy(b):
        return rdma(
            half.at[b, :, pl.ds(0, wide)], bl_got.at[b], bl_s.at[b], bl_r.at[b], tensor=1 - x
        )

    def bb_copy(b):
        return rdma(
            half.at[b, pl.ds(pl.multiple_of((1 - x) * four, four), four), pl.ds(wide, 2 * unit)],
            bb_got.at[b], bb_s.at[b], bb_r.at[b], tensor=1 - x,
        )

    def c_copy(b):
        return rdma(lat.at[b, pl.ds(mine, two)], lat.at[b, pl.ds(mine, two)], c_s.at[b], c_r.at[b], inner=1 - c)

    quarter = c * 2 + x

    def base_copy(b, e):
        return rdma(
            piece.at[b], base_all.at[b, pl.ds(pl.multiple_of(quarter * four, four), four)],
            base_s.at[b, e], base_r.at[b, quarter], expert=e, tensor=me // 2, inner=lax.rem(me, 2),
        )

    for load in loads:
        load.wait()

    bit = unit // 2 // cuts

    def span(w, half_at):
        return pl.ds(pl.multiple_of(half_at * (unit // 2) + w * bit, bit), bit)

    def w_right(b, w, src):
        return rdma(src, down_w.at[b, span(w, y)], wr_s.at[b, w], w_got.at[b, w], expert=lax.rem(me + 1, n))

    def w_left(b, w, src):
        return rdma(src, down_w.at[b, span(w, y)], wl_s.at[b, w], w_got.at[b, w], expert=lax.rem(me + n - 1, n))

    def w_side(b, w):
        spot = down_w.at[b, span(w, y)]
        return rdma(spot, spot, wy_s.at[b, w], wy_got.at[b, w], groups=1 - y)

    def w_side_wait(b):
        for w in range(cuts):
            spot = down_w.at[b, span(w, 1 - y)]
            rdma(spot, spot, wy_s.at[b, w], wy_got.at[b, w], groups=1 - y).wait_recv()

    def reach(k):
        d = nearest(me, jnp.minimum(k, n - 1), n) - me
        return jnp.where(k >= n, n, jnp.maximum(d, -d))

    def w_begin(k):
        now, before = reach(k), reach(jnp.maximum(k - 1, 0))

        @pl.when((me + 1 < n) & (now >= me + 1) & (before < me + 1))
        def _():
            for w in range(cuts):
                w_right(me, w, down_w.at[me, span(w, y)]).start()

        @pl.when((me >= 1) & (now >= n - me) & (before < n - me))
        def _():
            for w in range(cuts):
                w_left(me, w, down_w.at[me, span(w, y)]).start()

    def w_step(dist):
        for w in range(cuts):
            @pl.when(me >= dist)
            def _():
                b = lax.rem(me - dist + n, n)
                spot = down_w.at[b, span(w, y)]
                w_right(b, w, spot).wait_recv()

                @pl.when(me + 1 < n)
                def _():
                    w_right(b, w, spot).start()

                w_side(b, w).start()

            @pl.when(me + dist < n)
            def _():
                b = lax.rem(me + dist, n)
                spot = down_w.at[b, span(w, y)]
                w_left(b, w, spot).wait_recv()

                @pl.when(me >= 1)
                def _():
                    w_left(b, w, spot).start()

                w_side(b, w).start()

    def phase(k, carry):
        b = nearest(me, jnp.minimum(k, n - 1), n)

        @pl.when(k < n)
        def _():
            @pl.when(k >= 1)
            def _():
                to_right(b, all_tok.at[b]).wait_recv()

                @pl.when((b < me) & (me + 1 < n))
                def _():
                    to_right(b, all_tok.at[b]).start()

                @pl.when((b > me) & (me >= 1))
                def _():
                    to_left(b, all_tok.at[b]).start()

            w_begin(k)
            t = all_tok[b]
            nt = (((1,), (1,)), ((), ()))
            value = lax.dot_general(t, in_w[...], nt, preferred_element_type=F32).astype(BF16)
            if wide > packed:
                part[b, :, packed:wide] = jnp.zeros((rows, wide - packed), BF16)
            part[b, :, 0:packed] = value
            for g in range(2):
                value = lax.dot_general(t, base_w[g], nt, preferred_element_type=F32)
                part[b, :, wide + g * unit : wide + (g + 1) * unit] = value.astype(BF16)
            a_copy(b).start()

        @pl.when(k == n)
        def _():
            w_begin(n)

        @pl.when(k == n + 1)
        def _():
            w_step(1)

        @pl.when((k >= 1) & (k <= n))
        def _():
            p = nearest(me, jnp.maximum(k - 1, 0), n)
            bb_copy(p).wait_recv()
            own = half[p, pl.ds(pl.multiple_of(x * four, four), four), wide : wide + 2 * unit]
            piece[p] = (own.astype(F32) + bb_got[p].astype(F32)).astype(BF16)
            for e in range(n):
                here = (me == e) & (ti == me)

                @pl.when(jnp.logical_not(here))
                def _():
                    base_copy(p, e).start()

                @pl.when(here)
                def _():
                    base_all[p, pl.ds(pl.multiple_of(quarter * four, four), four)] = piece[p]

            bl_copy(p).wait_recv()
            lat[p, pl.ds(mine, two)] = (
                half[p, :, 0:wide].astype(F32) + bl_got[p].astype(F32)
            ).astype(BF16)
            c_copy(p).start()

        @pl.when(k < n)
        def _():
            a_copy(b).wait_recv()
            half[b] = (part[b, pl.ds(mine, two)].astype(F32) + a_got[b].astype(F32)).astype(BF16)
            bb_copy(b).start()
            bl_copy(b).start()

        @pl.when(k >= 2)
        def _():
            p = nearest(me, jnp.maximum(k - 2, 0), n)
            rdma(
                lat.at[p, pl.ds(other, two)], lat.at[p, pl.ds(other, two)], c_s.at[p], c_r.at[p],
                inner=1 - c,
            ).wait_recv()
            value = lat[p, :, 0:packed]
            for j in range(local):
                own = value * mask[j : j + 1, :].astype(BF16)
                for g in range(2):
                    delta[p, j, :, g * hid : (g + 1) * hid] = jnp.dot(
                        own, out_w[g], preferred_element_type=F32
                    ).astype(BF16)

        return carry

    lax.fori_loop(0, n + 2, phase, 0)

    for step in range(1, n):
        p = lax.rem(me + step, n)
        rdma(own_gates.at[p], own_gates.at[p], gate_s.at[p], gate_r.at[p], expert=p).wait_recv()

    def comb_copy(b):
        return rdma(comb.at[b], comb_got.at[me], comb_s.at[b], comb_r.at[me], expert=b)

    def finish(k, carry):
        b = nearest(ti, k, n)
        for q in range(plane):
            @pl.when(jnp.logical_not((me == ti) & (quarter == q)))
            def _():
                spot = base_all.at[b, pl.ds(q * four, four)]
                rdma(spot, spot, base_s.at[b, 0], base_r.at[b, q], tensor=1 - x).wait_recv()

        pick = (
            lax.broadcasted_iota(jnp.int32, (local, 128), 0)
            == lax.broadcasted_iota(jnp.int32, (local, 128), 1)
        ).astype(F32)
        weight = lax.dot_general(
            own_gates[b], pick, (((0,), (0,)), ((), ())),
            preferred_element_type=F32, precision=lax.Precision.HIGHEST,
        )
        gate_base = base_all[b, :, 0:unit].astype(F32)
        up_base = base_all[b, :, unit : 2 * unit].astype(F32)
        total = jnp.zeros((rows, hid), F32)
        for j in range(local):
            v = gate_base + delta[b, j, :, 0:hid].astype(F32)
            u = up_base + delta[b, j, :, hid : 2 * hid].astype(F32)
            total = total + weight[:, j : j + 1] * (v * (0.5 + 0.5 * jnp.tanh(0.5 * v)) * u)
        comb[b] = total.astype(BF16)

        @pl.when(b != me)
        def _():
            comb_copy(b).start()

        return carry

    middle = (me >= 1) & (me + 1 < n)

    def w_middle():
        for dist in range(2, n - 1):
            w_step(dist)

    pl.when(middle)(w_middle)
    lax.fori_loop(0, n - 1, finish, 0)
    pl.when(jnp.logical_not(middle))(w_middle)
    finish(n - 1, 0)

    total = comb[me].astype(F32)
    for step in range(1, n):
        p = lax.rem(me + step, n)
        rdma(comb_got.at[p], comb_got.at[p], comb_s.at[p], comb_r.at[p], expert=p).wait_recv()
        total = total + comb_got[p].astype(F32)
    full[ti] = total.astype(BF16)

    def ag_copy(step):
        to = lax.rem(ti + step, plane)
        return rdma(
            full.at[ti], full.at[ti], ag_s.at[to], ag_r.at[ti], tensor=to // 2, inner=lax.rem(to, 2)
        )

    for step in range(1, plane):
        ag_copy(step).start()
    for step in range(1, plane):
        p = lax.rem(ti + step, plane)
        rdma(full.at[p], full.at[p], ag_s.at[p], ag_r.at[p], tensor=1 - x).wait_recv()
    acc[...] = jnp.dot(full[me], down_w[me], preferred_element_type=F32)
    if n > 2:
        w_step(n - 1)
    for k in range(1, n):
        b = nearest(me, k, n)
        w_side_wait(b)
        acc[...] += jnp.dot(full[b], down_w[b], preferred_element_type=F32)
    out[...] = acc[...].astype(BF16)

    for b in range(n):
        @pl.when((b <= me) & (me + 1 < n))
        def _():
            to_right(b, all_tok.at[b]).wait_send()

        @pl.when((b >= me) & (me >= 1))
        def _():
            to_left(b, all_tok.at[b]).wait_send()

        a_copy(b).wait_send()
        bl_copy(b).wait_send()
        bb_copy(b).wait_send()
        c_copy(b).wait_send()
        for e in range(n):
            @pl.when(jnp.logical_not((me == e) & (ti == me)))
            def _():
                base_copy(b, e).wait_send()

        @pl.when(b != me)
        def _():
            comb_copy(b).wait_send()
            for w in range(cuts):
                w_side(b, w).wait_send()

        for w in range(cuts):
            @pl.when((b <= me) & (me + 1 < n))
            def _():
                w_right(b, w, down_w.at[b, span(w, y)]).wait_send()

            @pl.when((b >= me) & (me >= 1))
            def _():
                w_left(b, w, down_w.at[b, span(w, y)]).wait_send()

    for step in range(1, n):
        gate_copy(step).wait_send()
    for step in range(1, plane):
        ag_copy(step).wait_send()


def layer(tokens, dense_gates, base_weights, in_factor, out_factors, ranks):
    rows, feat = tokens.shape
    n = lax.axis_size("expert")
    plane = lax.axis_size("tensor") * lax.axis_size("inner")
    local = ranks.shape[0]
    packed = in_factor.shape[0]
    wide = -(-packed // 128) * 128
    unit = base_weights.shape[1]
    hid = out_factors.shape[2]
    order = lax.broadcasted_iota(jnp.int32, (local, local), 0)
    other = lax.broadcasted_iota(jnp.int32, (local, local), 1)
    ends = jnp.sum(jnp.where(other <= order, ranks[None, :], 0), axis=1)[:, None]
    place = lax.broadcasted_iota(jnp.int32, (local, packed), 1)
    mask = ((place < ends) & (place >= ends - ranks[:, None])).astype(F32)
    two, four = rows // 2, rows // 4
    cuts = 4
    vmem = pltpu.VMEM
    dma = pltpu.SemaphoreType.DMA
    return pl.pallas_call(
        functools.partial(fused, n, plane),
        out_shape=jax.ShapeDtypeStruct((rows, feat), BF16),
        in_specs=[
            pl.BlockSpec(memory_space=pl.ANY),
            pl.BlockSpec(memory_space=vmem),
            pl.BlockSpec(memory_space=vmem),
            pl.BlockSpec(memory_space=pl.ANY),
            pl.BlockSpec(memory_space=pl.ANY),
            pl.BlockSpec(memory_space=pl.ANY),
        ],
        out_specs=pl.BlockSpec(memory_space=vmem),
        scratch_shapes=[
            vmem((n, rows, feat), BF16),
            vmem((2, unit, feat), BF16),
            vmem((packed, feat), BF16),
            vmem((2, packed, hid), BF16),
            vmem((n, local, rows), F32),
            vmem((n, rows, wide + 2 * unit), BF16),
            vmem((n, two, wide + 2 * unit), BF16),
            vmem((n, two, wide + 2 * unit), BF16),
            vmem((n, two, wide), BF16),
            vmem((n, four, 2 * unit), BF16),
            vmem((n, rows, wide), BF16),
            vmem((n, four, 2 * unit), BF16),
            vmem((n, rows, 2 * unit), BF16),
            vmem((n, local, rows, 2 * hid), BF16),
            vmem((n, rows, hid), BF16),
            vmem((n, rows, hid), BF16),
            vmem((plane, rows, hid), BF16),
            vmem((n, unit, feat), BF16),
            vmem((rows, feat), F32),
            dma((6,)),
            dma((n,)), dma((n,)), dma((n,)), dma((n,)), dma((n,)),
            dma((n,)), dma((n,)), dma((n,)), dma((n,)), dma((n,)), dma((n,)), dma((n,)), dma((n,)),
            dma((n, n)), dma((n, plane)), dma((n,)), dma((n,)), dma((plane,)), dma((plane,)),
            dma((n, cuts)), dma((n, cuts)), dma((n, cuts)), dma((n, cuts)), dma((n, cuts)),
        ],
        compiler_params=pltpu.CompilerParams(
            collective_id=0, has_side_effects=True, vmem_limit_bytes=60 * 1024 * 1024
        ),
        cost_estimate=pl.CostEstimate(
            flops=60_000_000_000, bytes_accessed=20_000_000, transcendentals=0
        ),
    )(tokens, dense_gates.T, mask, base_weights, in_factor, out_factors)


def on_device(tokens, expert_ids, gate_weights, base_weights, in_factor, out_factors, ranks):
    tok_rows, feat_slice = tokens.shape
    owners = lax.axis_size("expert")
    local_count = ranks.shape[0]
    experts = local_count * owners
    packed = in_factor.shape[0]
    hidden_rows = base_weights.shape[1]
    hidden_slice = out_factors.shape[2]
    rows = tok_rows * owners

    columns = lax.broadcasted_iota(jnp.int32, (1, 1, experts), 2)
    chosen = expert_ids[:, :, None] == columns
    dense_gates = jnp.sum(jnp.where(chosen, gate_weights[:, :, None], 0.0), axis=1)
    tensor, inner = lax.axis_size("tensor"), lax.axis_size("inner")
    square = tensor == 2 and inner == 2 and owners == tensor * inner
    if square and lax.axis_size("groups") == 2 and tok_rows % 64 == 0 and hidden_rows % 128 == 0:
        return layer(tokens, dense_gates, base_weights, in_factor, out_factors, ranks)
    down = lax.all_gather(base_weights[2], "expert", axis=0, tiled=True)
    all_tokens = lax.all_gather(tokens, "expert", axis=0, tiled=True)
    all_gates = lax.all_gather(dense_gates, "expert", axis=0, tiled=True)
    own_gates = lax.dynamic_slice_in_dim(
        all_gates, lax.axis_index("expert") * local_count, local_count, 1
    )

    latent_part = lax.dot_general(
        all_tokens, in_factor, (((1,), (1,)), ((), ())), preferred_element_type=jnp.float32
    ).astype(jnp.bfloat16)
    latent = lax.psum(latent_part, FEATURE_AXES)

    base_part = lax.dot_general(
        all_tokens,
        base_weights[:2].reshape(2 * hidden_rows, feat_slice),
        (((1,), (1,)), ((), ())),
        preferred_element_type=jnp.float32,
    ).astype(jnp.bfloat16)
    base = lax.psum_scatter(base_part, FEATURE_AXES, scatter_dimension=0, tiled=True)
    base = base.reshape(-1, 2, hidden_rows)
    base = lax.all_gather(base, "expert", axis=2, tiled=True)
    base = lax.all_to_all(base, FEATURE_AXES, split_axis=2, concat_axis=0, tiled=True)
    gate_rows = base[:, 0].astype(jnp.float32)
    up_rows = base[:, 1].astype(jnp.float32)

    order = lax.broadcasted_iota(jnp.int32, (local_count, local_count), 0)
    other = lax.broadcasted_iota(jnp.int32, (local_count, local_count), 1)
    ends = jnp.sum(jnp.where(other <= order, ranks[None, :], 0), axis=1)
    where = lax.broadcasted_iota(jnp.int32, (1, packed), 1)
    combined = jnp.zeros((rows, hidden_slice), jnp.float32)
    for member in range(local_count):
        inside = (where >= ends[member] - ranks[member]) & (where < ends[member])
        own = jnp.where(inside, latent, jnp.zeros((), jnp.bfloat16))
        gate = jnp.dot(own, out_factors[0], preferred_element_type=jnp.float32)
        up = jnp.dot(own, out_factors[1], preferred_element_type=jnp.float32)
        hidden = jax.nn.silu(gate_rows + gate) * (up_rows + up)
        combined = combined + own_gates[:, member : member + 1] * hidden
    combined = lax.psum_scatter(
        combined.astype(jnp.bfloat16), "expert", scatter_dimension=0, tiled=True
    )
    full_hidden = lax.all_gather(combined, FEATURE_AXES, axis=1, tiled=True)
    return jnp.dot(full_hidden, down, preferred_element_type=jnp.float32).astype(jnp.bfloat16)


def solution(mesh):
    return jax.shard_map(
        on_device,
        mesh=mesh,
        in_specs=(
            P(("groups", "expert"), ("tensor", "inner")),
            P(("groups", "expert"), None),
            P(("groups", "expert"), None),
            P(None, "expert", ("tensor", "inner")),
            P("expert", ("tensor", "inner")),
            P(None, "expert", ("tensor", "inner")),
            P("expert"),
        ),
        out_specs=P(("groups", "expert"), ("tensor", "inner")),
        check_vma=False,
    )
```
